256 devices in a mesh: blk: 64 (over z, y, x_hi), grp: 4 (over x_lo, core).
Axes of the slice: x: 4 (x_hi: 2, x_lo: 2; x = x_hi * 2 + x_lo), y: 4, z: 8, core: 2. Of those that a mesh axis runs over, the one named last changes fastest.
Arguments:
- embeddings: float32 [98304, 1024], P(('blk', 'grp')), may hold values from -0.25 to 0.25
- normalizers: bfloat16 [98304], P(('blk', 'grp')), may hold values from 2 to 5
- partner_index: int32 [98304], P(('blk', 'grp')), may hold values from 0 to 98303, as said below
Outputs:
- grad_embeddings: float32 [98304, 1024], P(('blk', 'grp'))
The draws below stay inside these ranges and needn't reach their ends.
Inputs may be any that keep to these rules, and one draw needn't show every extreme that they name: partner_index[partner_index[i]] = i and partner_index[i] != i; each view's partner lies in the same row block of 1536 views (same i // 1536).
All inputs are finite; a program needn't handle non-finite values.
Results may differ from the reference program's by a relative error of at most 0.0046.
Values may be sent and summed in bfloat16 or wider, within the bound.
A program may use at most 128 MiB of HBM per device.

```python
import jax
import jax.numpy as jnp
from jax import lax

D = 1024
ROUNDS = 2
BLOCK_ROWS = 1536
VIEWS = 98304


def draw_partner_index(key, part):
    key = jax.random.fold_in(key, 11)
    block_count = VIEWS // BLOCK_ROWS
    block_keys = jax.random.split(key, block_count)

    def pair_block(block_key, block_number):
        order = jax.random.permutation(block_key, BLOCK_ROWS).astype(jnp.int32)
        firsts = order[0::2]
        seconds = order[1::2]
        local = jnp.zeros((BLOCK_ROWS,), jnp.int32).at[firsts].set(seconds).at[seconds].set(firsts)
        return local + block_number * BLOCK_ROWS
    paired = jax.vmap(pair_block)(block_keys, jnp.arange(block_count, dtype=jnp.int32))
    return paired.reshape(VIEWS).astype(jnp.int32)


def steps_of(own_key, extent, shards, smallest, high):
    loudness, own = 1.0, jax.random.fold_in(own_key, 6)
    for dim, parts in shards:
        draws = jnp.exp(jax.random.uniform(jax.random.fold_in(own, dim), (parts,), jnp.float32, smallest / len(shards), high / len(shards)))
        loudness = loudness * jnp.repeat(draws, extent[dim] // parts).reshape([-1 if axis == dim else 1 for axis in range(len(extent))])
    return loudness


def gaussian(rng, extent, scale, limit, cuts=(), held_as=jnp.bfloat16):
    result = jax.random.normal(rng, extent, jnp.float32) * scale
    if len(cuts) > 0:
        result = steps_of(rng, extent, cuts, -0.22, 0.18) * result
    return jnp.clip(result, min=-limit, max=limit).astype(held_as)


def setup_inputs(seed: int = 0) -> dict:
    keys = jax.random.split(jax.random.key(seed), 4)
    embeddings = gaussian(keys[0], (VIEWS, D), 0.03125, 0.25, ((0, 256),), jnp.float32)
    normalizers = jnp.clip(2.0 + 3.0 * jax.random.uniform(keys[1], (VIEWS,), jnp.float32) ** steps_of(keys[1], (VIEWS,), ((0, 256),), -0.2, 0.2), 2.0, 5.0).astype(jnp.bfloat16)
    partner_index = draw_partner_index(jax.random.fold_in(keys[3], 71), 0)
    return dict(embeddings=embeddings, normalizers=normalizers, partner_index=partner_index)


inverse_temp = 10.0

def pair_weights(scores, left_norm, right_norm):
    return (jnp.exp(scores - left_norm[:, None]) + jnp.exp(scores - right_norm[None, :])).astype(jnp.bfloat16)

def reference(embeddings, normalizers, partner_index):
    inv_norm = lax.rsqrt(lax.optimization_barrier(jnp.sum(embeddings * embeddings, axis=1, keepdims=True)) + 1e-06)
    normed = embeddings * inv_norm
    rounded = normed.astype(jnp.bfloat16)
    block_count = VIEWS // BLOCK_ROWS
    block_units = rounded.reshape(block_count, BLOCK_ROWS, D)
    block_norms = normalizers.astype(jnp.float32).reshape(block_count, BLOCK_ROWS)

    def pull_block(block_number):
        resident = block_units[block_number]
        resident_norm = block_norms[block_number]
        summed = jnp.zeros((BLOCK_ROWS, D), jnp.float32)
        for offset in list(range(1, ROUNDS + 1)) + list(range(-ROUNDS, 0)):
            partner_block = (block_number - offset) % block_count
            guests = block_units[partner_block]
            guest_norm = block_norms[partner_block]
            scores = jnp.dot(resident, guests.T, preferred_element_type=jnp.float32) * inverse_temp
            weights = pair_weights(scores, resident_norm, guest_norm)
            summed = summed + jnp.dot(weights, guests, preferred_element_type=jnp.float32)
        return summed
    pulled = lax.map(pull_block, jnp.arange(block_count, dtype=jnp.int32)).reshape(VIEWS, D)
    positive = jnp.take(rounded, partner_index, axis=0).astype(jnp.float32)
    grad_unit = inverse_temp * (pulled - 2.0 * positive)
    radial = lax.optimization_barrier(jnp.sum(normed * grad_unit, axis=1, keepdims=True))
    return inv_norm * (grad_unit - normed * radial)
```

```python
import functools

import jax
import jax.numpy as jnp
from jax import lax
from jax.experimental import pallas as pl
from jax.experimental.pallas import tpu as pltpu
from jax.sharding import PartitionSpec as P

MESH = pl.DeviceIdType.MESH
ROWS = 384
D = 1024
K = 6
R = ROWS // K
T = 128
TILES = ROWS // T
INV_TEMP = 10.0
SCALE = INV_TEMP * 1.4426950408889634


def tile_of(row):
    pieces = [row[:, k * R : (k + 1) * R] for k in range(K)]
    body = jnp.concatenate(pieces + [jnp.zeros((8 - K, R), row.dtype)], axis=0)
    return jnp.concatenate([body, jnp.zeros((8, 128 - R), row.dtype)], axis=1)


def columns_of(tile):
    turned = jnp.transpose(jnp.concatenate([tile] * 16, axis=0))
    return jnp.concatenate(
        [jnp.broadcast_to(turned[0:R, k : k + 1], (R, 128)) for k in range(K)], axis=0
    )


def kernel(
    blocks, emb_hbm, norm_ref, partner_ref, out_ref,
    emb, invs, block, ga, gb, relay, acc_own, acc_pair, part_out, part_in,
    e_own, e_pair, e_a, e_relay, e_b, col_own, col_pair,
    emb_sem, sib_s, sib_r, own_s, own_r, siba_s, siba_r, fwd_s, fwd_r, rel_s, rel_r,
    out_s, out_r, sibb_s, sibb_r, part_s, part_r, e_s, e_r,
):
    blk = lax.axis_index("blk")
    grp = lax.axis_index("grp")
    x_hi = blk % 2
    x_lo = grp // 2
    core = grp % 2
    turn = 2 * (1 - 2 * x_hi)
    pair_grp = (1 - x_lo) * 2 + core
    sib = (blk, x_lo * 2 + 1 - core)
    pair = (blk, pair_grp)
    outer = (blk + 1 - 2 * x_hi, pair_grp)
    ahead = ((blk + turn + blocks) % blocks, grp)
    behind = ((blk - turn + blocks) % blocks, grp)

    def remote(src, dst, send, recv, to):
        return pltpu.make_async_remote_copy(
            src_ref=src, dst_ref=dst, send_sem=send, recv_sem=recv, device_id=to, device_id_type=MESH
        )

    load = pltpu.make_async_copy(emb_hbm, emb, emb_sem)
    load.start()
    barrier = pltpu.get_barrier_semaphore()
    neighbours = (sib, pair, outer, ahead, behind)
    for to in neighbours:
        pl.semaphore_signal(barrier, inc=1, device_id=to, device_id_type=MESH)

    e_tile = tile_of(jnp.exp(-norm_ref[...].astype(jnp.float32)))
    e_own[...] = e_tile
    col_own[...] = columns_of(e_tile)
    load.wait()

    def normalize(t, _):
        at = pl.ds(pl.multiple_of(t * R, R), R)
        x = emb[at, :]
        inv = lax.rsqrt(jnp.sum(x * x, axis=1, keepdims=True) + 1e-06)
        invs[at, :] = jnp.broadcast_to(inv, (R, 128))
        block[grp, at, :] = (x * inv).astype(jnp.bfloat16)
        acc_own[at, :] = jnp.zeros((R, D), jnp.float32)
        acc_pair[at, :] = jnp.zeros((R, D), jnp.float32)
        return 0

    lax.fori_loop(0, K, normalize, 0)
    pl.semaphore_wait(barrier, len(neighbours))

    def lane_a(c, stream, n=1):
        return pl.ds(pl.multiple_of((c * 3 + stream) * R, R), n * R)

    def lane_b(c, stream, n=1):
        return pl.ds(pl.multiple_of((c * 2 + stream) * R, R), n * R)

    def piece(k):
        return pl.ds(pl.multiple_of(k * R, R), R)

    e_copies = [
        remote(e_own, e_pair, e_s.at[0], e_r.at[0], pair),
        remote(e_own, e_a.at[core, 0], e_s.at[1], e_r.at[1], outer),
        remote(e_own, e_a.at[core, 1], e_s.at[2], e_r.at[2], behind),
        remote(e_own, e_a.at[core, 2], e_s.at[3], e_r.at[3], ahead),
    ]
    e_sib = remote(e_a.at[core], e_a.at[core], e_s.at[4], e_r.at[4], sib)
    e_sib_in = remote(e_a.at[1 - core], e_a.at[1 - core], e_s.at[4], e_r.at[4], sib)
    e_fwd = remote(e_a.at[core, 0], e_b.at[core, 0], e_s.at[5], e_r.at[5], ahead)
    e_rel = remote(e_pair, e_relay, e_s.at[6], e_r.at[6], behind)
    e_out = remote(e_relay, e_b.at[core, 1], e_s.at[7], e_r.at[7], outer)
    e_sibb = remote(e_b.at[core], e_b.at[core], e_s.at[8], e_r.at[8], sib)
    e_sibb_in = remote(e_b.at[1 - core], e_b.at[1 - core], e_s.at[8], e_r.at[8], sib)

    def own_pair(k):
        return remote(block.at[grp, piece(k)], block.at[grp, piece(k)], own_s.at[0, k], own_r.at[0, k], pair)

    def pair_in(k):
        at = block.at[pair_grp, piece(k)]
        return remote(at, at, own_s.at[0, k], own_r.at[0, k], pair)

    def own_to(k, stream, to):
        return remote(
            block.at[grp, piece(k)], ga.at[k, lane_a(core, stream)],
            own_s.at[1 + stream, k], own_r.at[1 + stream, k], to,
        )

    def sib_a(k):
        at = ga.at[k, lane_a(core, 0, 3)]
        return remote(at, at, siba_s.at[k], siba_r.at[k], sib)

    def sib_a_in(k):
        at = ga.at[k, lane_a(1 - core, 0, 3)]
        return remote(at, at, siba_s.at[k], siba_r.at[k], sib)

    def fwd(k):
        return remote(ga.at[k, lane_a(core, 0)], gb.at[k, lane_b(core, 0)], fwd_s.at[k], fwd_r.at[k], ahead)

    def rel(k):
        return remote(block.at[pair_grp, piece(k)], relay.at[k], rel_s.at[k], rel_r.at[k], behind)

    def rel_out(k):
        return remote(relay.at[k], gb.at[k, lane_b(core, 1)], out_s.at[k], out_r.at[k], outer)

    def sib_b(k):
        at = gb.at[k, lane_b(core, 0, 2)]
        return remote(at, at, sibb_s.at[k], sibb_r.at[k], sib)

    def sib_b_in(k):
        at = gb.at[k, lane_b(1 - core, 0, 2)]
        return remote(at, at, sibb_s.at[k], sibb_r.at[k], sib)

    def tile(t):
        return pl.ds(pl.multiple_of(t * T, T), T)

    def partial(t):
        return remote(part_out.at[tile(t)], part_in.at[tile(t)], part_s.at[t], part_r.at[t], pair)

    sib_own = remote(block.at[grp], block.at[grp], sib_s.at[0], sib_r.at[0], sib)
    sib_own_in = remote(block.at[sib[1]], block.at[sib[1]], sib_s.at[0], sib_r.at[0], sib)
    sib_pair = remote(block.at[pair_grp], block.at[pair_grp], sib_s.at[1], sib_r.at[1], sib)
    cross = (1 - x_lo) * 2 + 1 - core
    sib_pair_in = remote(block.at[cross], block.at[cross], sib_s.at[1], sib_r.at[1], sib)

    for copy in e_copies:
        copy.start()

    def send_own(k, _):
        own_pair(k).start()
        own_to(k, 0, outer).start()
        own_to(k, 1, behind).start()
        own_to(k, 2, ahead).start()
        return 0

    lax.fori_loop(0, K, send_own, 0)
    sib_own.start()

    for copy in e_copies:
        copy.wait_recv()
    e_sib.start()
    e_fwd.start()
    e_rel.start()
    col_pair[...] = columns_of(e_pair[...])
    e_sib_in.wait_recv()

    def pull(rows, col, guests, e_row):
        scores = lax.dot_general(
            rows, guests, (((1,), (1,)), ((), ())), preferred_element_type=jnp.float32
        )
        spread = jnp.concatenate([col] * (guests.shape[0] // 128), axis=1)
        weights = (jnp.exp2(scores * SCALE) * (spread + e_row)).astype(jnp.bfloat16)
        return jnp.dot(weights, guests, preferred_element_type=jnp.float32)

    def e_row_of(e, k, streams):
        return jnp.concatenate(
            [e[c, s, pl.ds(k, 1), 0:R] for c in range(2) for s in range(streams)], axis=1
        )

    def pair_job(t, k):
        acc_pair[tile(t), :] += pull(
            block[pair_grp, tile(t), :], col_pair[tile(t), :], ga[k], e_row_of(e_a, k, 3)
        )

    def send_partial(t):
        part_out[tile(t), :] = acc_pair[tile(t), :].astype(jnp.bfloat16)
        partial(t).start()

    def phase_one(k, _):
        @pl.when(k < K)
        def _():
            own_to(k, 0, outer).wait_recv()
            fwd(k).start()
            pair_in(k).wait_recv()
            rel(k).start()
            own_to(k, 1, behind).wait_recv()
            own_to(k, 2, ahead).wait_recv()
            sib_a(k).start()

        @pl.when(k > 0)
        def _():
            sib_a_in(k - 1).wait_recv()
            pair_job(0, k - 1)

            @pl.when(k == K)
            def _():
                send_partial(0)

            acc_own[...] += pull(block[grp], col_own[...], ga[k - 1], e_row_of(e_a, k - 1, 3))

        return 0

    lax.fori_loop(0, K + 1, phase_one, 0)
    sib_pair.start()
    e_rel.wait_recv()
    e_out.start()

    def pass_on(k):
        rel(k).wait_recv()
        rel_out(k).start()

    def pair_tiles(t, _):
        pass_on(t - 1)

        def step(k, _):
            pair_job(t, k)
            return 0

        lax.fori_loop(0, K, step, 0)
        send_partial(t)
        return 0

    lax.fori_loop(1, TILES, pair_tiles, 0)
    for k in range(TILES - 1, 3):
        pass_on(k)

    sib_own_in.wait_recv()
    sib_pair_in.wait_recv()
    local = partner_ref[...] - blk * (4 * ROWS)
    local = columns_of(tile_of(local.astype(jnp.float32))).astype(jnp.int32)
    local = jnp.concatenate([local] * (ROWS // 128), axis=1)
    lanes = lax.broadcasted_iota(jnp.int32, (ROWS, ROWS), 1)

    def positive(g, _):
        chosen = jnp.where(local == lanes + g * ROWS, -2.0, 0.0).astype(jnp.bfloat16)
        acc_own[...] += jnp.dot(chosen, block[g], preferred_element_type=jnp.float32)
        return 0

    lax.fori_loop(0, 4, positive, 0)

    e_fwd.wait_recv()
    e_out.wait_recv()
    e_sibb.start()
    e_sibb_in.wait_recv()

    def phase_two(k, _):
        @pl.when(k < K)
        def _():
            fwd(k).wait_recv()
            rel_out(k).wait_recv()
            sib_b(k).start()

        @pl.when(k < K - 3)
        def _():
            pass_on(k + 3)

        @pl.when(k > 0)
        def _():
            sib_b_in(k - 1).wait_recv()
            acc_own[...] += pull(block[grp], col_own[...], gb[k - 1], e_row_of(e_b, k - 1, 2))

        return 0

    lax.fori_loop(0, K + 1, phase_two, 0)

    def finish(t, _):
        partial(t).wait_recv()
        at = tile(t)
        inv = invs[at, 0:1]
        normed = emb[at, :] * inv
        unit = INV_TEMP * (acc_own[at, :] + part_in[at, :].astype(jnp.float32))
        radial = jnp.sum(normed * unit, axis=1, keepdims=True)
        out_ref[at, :] = inv * (unit - normed * radial)
        return 0

    lax.fori_loop(0, TILES, finish, 0)

    def drain(k, _):
        own_pair(k).wait_send()
        own_to(k, 0, outer).wait_send()
        own_to(k, 1, behind).wait_send()
        own_to(k, 2, ahead).wait_send()
        sib_a(k).wait_send()
        fwd(k).wait_send()
        rel(k).wait_send()
        rel_out(k).wait_send()
        sib_b(k).wait_send()
        return 0

    lax.fori_loop(0, K, drain, 0)
    for t in range(TILES):
        partial(t).wait_send()
    for copy in e_copies + [e_sib, e_fwd, e_rel, e_out, e_sibb, sib_own, sib_pair]:
        copy.wait_send()


def solution(mesh):
    blocks = mesh.shape["blk"]
    bf16, f32 = jnp.bfloat16, jnp.float32
    dma = pltpu.SemaphoreType.DMA

    def per_device(embeddings, normalizers, partner_index):
        vmem = pl.BlockSpec(memory_space=pltpu.VMEM)
        return pl.pallas_call(
            functools.partial(kernel, blocks),
            out_shape=jax.ShapeDtypeStruct((ROWS, D), f32),
            in_specs=[pl.BlockSpec(memory_space=pl.ANY), vmem, vmem],
            out_specs=vmem,
            scratch_shapes=[
                pltpu.VMEM((ROWS, D), f32),
                pltpu.VMEM((ROWS, 128), f32),
                pltpu.VMEM((4, ROWS, D), bf16),
                pltpu.VMEM((K, 6 * R, D), bf16),
                pltpu.VMEM((K, 4 * R, D), bf16),
                pltpu.VMEM((K, R, D), bf16),
                pltpu.VMEM((ROWS, D), f32),
                pltpu.VMEM((ROWS, D), f32),
                pltpu.VMEM((ROWS, D), bf16),
                pltpu.VMEM((ROWS, D), bf16),
                pltpu.VMEM((8, 128), f32),
                pltpu.VMEM((8, 128), f32),
                pltpu.VMEM((2, 3, 8, 128), f32),
                pltpu.VMEM((8, 128), f32),
                pltpu.VMEM((2, 2, 8, 128), f32),
                pltpu.VMEM((ROWS, 128), f32),
                pltpu.VMEM((ROWS, 128), f32),
                dma, dma((2,)), dma((2,)), dma((4, K)), dma((4, K)), dma((K,)), dma((K,)),
                dma((K,)), dma((K,)), dma((K,)), dma((K,)), dma((K,)), dma((K,)), dma((K,)), dma((K,)),
                dma((TILES,)), dma((TILES,)), dma((9,)), dma((9,)),
            ],
            compiler_params=pltpu.CompilerParams(
                collective_id=0, has_side_effects=True, vmem_limit_bytes=48 << 20
            ),
            cost_estimate=pl.CostEstimate(
                flops=10 * 10**9, bytes_accessed=4 << 20, transcendentals=3 * 10**6
            ),
        )(embeddings, normalizers.reshape(1, ROWS), partner_index.reshape(1, ROWS))

    placed = (P(("blk", "grp"), None), P(("blk", "grp")), P(("blk", "grp")))
    return jax.shard_map(
        per_device, mesh=mesh, in_specs=placed, out_specs=P(("blk", "grp"), None), check_vma=False
    )
```

```python
import functools

import jax
import jax.numpy as jnp
from jax import lax
from jax.experimental import pallas as pl
from jax.experimental.pallas import tpu as pltpu
from jax.sharding import PartitionSpec as P

MESH = pl.DeviceIdType.MESH
ROWS = 384
D = 1024
K = 6
R = ROWS // K
N2 = 12
R2 = ROWS // N2
T = 128
TILES = ROWS // T
INV_TEMP = 10.0
SCALE = INV_TEMP * 1.4426950408889634


def tile_of(row):
    pieces = [row[:, k * R : (k + 1) * R] for k in range(K)]
    body = jnp.concatenate(pieces + [jnp.zeros((8 - K, R), row.dtype)], axis=0)
    return jnp.concatenate([body, jnp.zeros((8, 128 - R), row.dtype)], axis=1)


def columns_of(tile):
    turned = jnp.transpose(jnp.concatenate([tile] * 16, axis=0))
    return jnp.concatenate(
        [jnp.broadcast_to(turned[0:R, k : k + 1], (R, 128)) for k in range(K)], axis=0
    )


def kernel(
    blocks, emb_hbm, norm_hbm, partner_hbm, out_ref,
    emb, norm, partner, invs, work, others, ga, gb1, gb2, relay, acc, part_out, part_in,
    e_own, e_pair, e_a, e_relay, e_b, col, row_a, row_b1, row_b2,
    load_s, small_s, sib_s, sib_r, own_s, own_r, siba_s, siba_r, fwd_s, fwd_r, rel_s, rel_r,
    out_s, out_r, sib1_s, sib1_r, sib2_s, sib2_r, part_s, part_r, e_s, e_r,
):
    blk = lax.axis_index("blk")
    grp = lax.axis_index("grp")
    x_hi = blk % 2
    x_lo = grp // 2
    core = grp % 2
    turn = 2 * (1 - 2 * x_hi)
    pair_grp = (1 - x_lo) * 2 + core
    sib_grp = x_lo * 2 + 1 - core
    cross_grp = (1 - x_lo) * 2 + 1 - core
    sib = (blk, sib_grp)
    pair = (blk, pair_grp)
    outer = (blk + 1 - 2 * x_hi, pair_grp)
    ahead = ((blk + turn + blocks) % blocks, grp)
    behind = ((blk - turn + blocks) % blocks, grp)

    def remote(src, dst, send, recv, to):
        return pltpu.make_async_remote_copy(
            src_ref=src, dst_ref=dst, send_sem=send, recv_sem=recv, device_id=to, device_id_type=MESH
        )

    def rows(at, n):
        return pl.ds(at, n)

    def laned(at, c, n):
        return pl.ds(pl.multiple_of(at + c * n, 16), n)

    def lane_a(k, stream):
        return pl.ds(pl.multiple_of((k * 6 + stream + core * 3) * R, 16), R)

    loads = [
        pltpu.make_async_copy(emb_hbm.at[rows(k * R, R)], emb.at[rows(k * R, R)], load_s.at[k])
        for k in range(K)
    ]
    small = [
        pltpu.make_async_copy(norm_hbm, norm, small_s.at[0]),
        pltpu.make_async_copy(partner_hbm, partner, small_s.at[1]),
    ]
    small[0].start()
    for copy in loads:
        copy.start()
    small[1].start()
    barrier = pltpu.get_barrier_semaphore()
    neighbours = (sib, pair, outer, ahead, behind)
    for to in neighbours:
        pl.semaphore_signal(barrier, inc=1, device_id=to, device_id_type=MESH)

    small[0].wait()
    e_tile = tile_of(jnp.exp(-norm[...].astype(jnp.float32)).reshape(1, ROWS))
    e_own[...] = e_tile

    def normalize(k):
        loads[k].wait()
        at = rows(k * R, R)
        x = emb[at, :]
        inv = lax.rsqrt(jnp.sum(x * x, axis=1, keepdims=True) + 1e-06)
        invs[at, :] = jnp.broadcast_to(inv, (R, 128))
        work[at, :] = (x * inv).astype(jnp.bfloat16)

    e_copies = [
        remote(e_own, e_pair, e_s.at[0], e_r.at[0], pair),
        remote(e_own, e_a.at[core, 0], e_s.at[1], e_r.at[1], outer),
        remote(e_own, e_a.at[core, 1], e_s.at[2], e_r.at[2], behind),
        remote(e_own, e_a.at[core, 2], e_s.at[3], e_r.at[3], ahead),
    ]
    e_sib = remote(e_a.at[core], e_a.at[core], e_s.at[4], e_r.at[4], sib)
    e_sib_in = remote(e_a.at[1 - core], e_a.at[1 - core], e_s.at[4], e_r.at[4], sib)
    e_fwd = remote(e_a.at[core, 0], e_b.at[core, 0], e_s.at[5], e_r.at[5], ahead)
    e_rel = remote(e_pair, e_relay, e_s.at[6], e_r.at[6], behind)
    e_out = remote(e_relay, e_b.at[core, 1], e_s.at[7], e_r.at[7], outer)
    e_sibb = remote(e_b.at[core], e_b.at[core], e_s.at[8], e_r.at[8], sib)
    e_sibb_in = remote(e_b.at[1 - core], e_b.at[1 - core], e_s.at[8], e_r.at[8], sib)

    own_pair = [
        remote(work.at[rows(k * R, R)], work.at[rows(ROWS + k * R, R)], own_s.at[0, k], own_r.at[0, k], pair)
        for k in range(K)
    ]

    def own_to(stream, to):
        return [
            remote(
                work.at[rows(k * R, R)], ga.at[lane_a(k, stream)],
                own_s.at[1 + stream, k], own_r.at[1 + stream, k], to,
            )
            for k in range(K)
        ]

    own_outer, own_behind, own_ahead = own_to(0, outer), own_to(1, behind), own_to(2, ahead)

    def both_ways(ref, at, n, send, recv):
        mine = ref.at[laned(at, core, n)]
        theirs = ref.at[laned(at, 1 - core, n)]
        return remote(mine, mine, send, recv, sib), remote(theirs, theirs, send, recv, sib)

    sib_a = [both_ways(ga, k * 6 * R, 3 * R, siba_s.at[k], siba_r.at[k]) for k in range(K)]
    sib_1 = [both_ways(gb1, k * 2 * R, R, sib1_s.at[k], sib1_r.at[k]) for k in range(K)]
    sib_2 = [both_ways(gb2, i * 2 * R2, R2, sib2_s.at[i], sib2_r.at[i]) for i in range(N2)]
    fwd = [
        remote(
            ga.at[lane_a(k, 0)],
            gb1.at[laned(k * 2 * R, core, R)], fwd_s.at[k], fwd_r.at[k], ahead,
        )
        for k in range(K)
    ]
    rel = [
        remote(work.at[rows(ROWS + i * R2, R2)], relay.at[rows(i * R2, R2)], rel_s.at[i], rel_r.at[i], behind)
        for i in range(N2)
    ]
    rel_out = [
        remote(relay.at[rows(i * R2, R2)], gb2.at[laned(i * 2 * R2, core, R2)], out_s.at[i], out_r.at[i], outer)
        for i in range(N2)
    ]
    partial = [
        remote(part_out.at[rows(t * T, T)], part_in.at[rows(t * T, T)], part_s.at[t], part_r.at[t], pair)
        for t in range(TILES)
    ]
    sib_own = remote(work.at[rows(0, ROWS)], others.at[0], sib_s.at[0], sib_r.at[0], sib)
    sib_pair = remote(work.at[rows(ROWS, ROWS)], others.at[1], sib_s.at[1], sib_r.at[1], sib)

    normalize(0)
    pl.semaphore_wait(barrier, len(neighbours))
    for copy in e_copies:
        copy.start()
    for k in range(K):
        own_pair[k].start()
        own_outer[k].start()
        own_behind[k].start()
        own_ahead[k].start()
        if k + 1 < K:
            normalize(k + 1)
    sib_own.start()
    col[0:ROWS, :] = columns_of(e_tile)

    for copy in e_copies:
        copy.wait_recv()
    e_sib.start()
    e_fwd.start()
    e_rel.start()
    col[ROWS : 2 * ROWS, :] = columns_of(e_pair[...])
    e_sib_in.wait_recv()
    row_a[0:1, :] = jnp.concatenate(
        [e_a[c, s, k : k + 1, 0:R] for k in range(K) for c in range(2) for s in range(3)], axis=1
    )

    def pull(r0, m, guests, row, g0, g, first=False):
        own, met = rows(r0, m), guests[rows(g0, g), :]
        scores = lax.dot_general(
            work[own, :], met, (((1,), (1,)), ((), ())), preferred_element_type=jnp.float32
        )
        spread = jnp.concatenate([col[own, :]] * (g // 128), axis=1) + row[0:1, g0 : g0 + g]
        weights = (jnp.exp2(scores * SCALE) * spread).astype(jnp.bfloat16)
        add = jnp.dot(weights, met, preferred_element_type=jnp.float32)
        acc[own, :] = add if first else acc[own, :] + add

    def pull_a(r0, m, k, n, first=False):
        pull(r0, m, ga, row_a, k * 6 * R, n * 6 * R, first)

    p0, p1, p2 = ROWS, ROWS + T, ROWS + 2 * T

    def arrive(k):
        own_outer[k].wait_recv()
        fwd[k].start()
        own_pair[k].wait_recv()
        rel[2 * k].start()
        rel[2 * k + 1].start()
        own_behind[k].wait_recv()
        own_ahead[k].wait_recv()
        sib_a[k][0].start()

    def send_partial(t):
        part_out[rows(t * T, T), :] = acc[rows(ROWS + t * T, T), :].astype(jnp.bfloat16)
        partial[t].start()

    def pass_on(i):
        rel[i].wait_recv()
        rel_out[i].start()

    small[1].wait()
    local = partner[...].reshape(1, ROWS) - blk * (4 * ROWS)
    local = columns_of(tile_of(local.astype(jnp.float32))).astype(jnp.int32)

    def positive(held, g):
        lanes = lax.broadcasted_iota(jnp.int32, (ROWS, ROWS), 1) + g * ROWS
        spread = jnp.concatenate([local] * (ROWS // 128), axis=1)
        chosen = jnp.where(spread == lanes, -2.0, 0.0).astype(jnp.bfloat16)
        acc[0:ROWS, :] += jnp.dot(chosen, held[...], preferred_element_type=jnp.float32)

    arrive(0)
    arrive(1)
    sib_a[0][1].wait_recv()
    sib_a[1][1].wait_recv()
    pull_a(0, ROWS + T, 0, 2, first=True)
    arrive(2)
    sib_own.wait_recv()
    positive(work.at[rows(0, ROWS)], grp)
    positive(others.at[0], sib_grp)
    arrive(3)
    pull_a(p1, T, 0, 2, first=True)
    sib_a[2][1].wait_recv()
    sib_a[3][1].wait_recv()
    pull_a(0, ROWS + T, 2, 2)
    arrive(4)
    pull_a(p1, T, 2, 2)
    arrive(5)
    sib_a[4][1].wait_recv()
    pull_a(p0, T, 4, 1)
    pull_a(p2, T, 0, 2, first=True)
    e_rel.wait_recv()
    e_out.start()
    pass_on(0)
    sib_a[5][1].wait_recv()
    pull_a(p0, T, 5, 1)
    send_partial(0)
    sib_pair.start()
    pass_on(1)
    pull_a(p1, T, 4, 2)
    send_partial(1)
    pass_on(2)
    pull_a(p2, T, 2, 2)
    pass_on(3)
    pull_a(p2, T, 4, 2)
    send_partial(2)
    pass_on(4)
    pull_a(0, ROWS, 4, 1)
    pass_on(5)
    pull_a(0, ROWS, 5, 1)
    pass_on(6)
    sib_pair.wait_recv()
    positive(work.at[rows(ROWS, ROWS)], pair_grp)
    positive(others.at[1], cross_grp)
    pass_on(7)

    def arrive_1(k):
        fwd[k].wait_recv()
        sib_1[k][0].start()

    def arrive_2(i):
        rel_out[i].wait_recv()
        sib_2[i][0].start()

    e_fwd.wait_recv()
    e_out.wait_recv()
    e_sibb.start()
    for k in range(3):
        arrive_1(k)
    for i in range(4):
        arrive_2(i)
    pass_on(8)
    e_sibb_in.wait_recv()
    row_b1[0:1, :] = jnp.concatenate(
        [e_b[c, 0, k : k + 1, 0:R] for k in range(K) for c in range(2)], axis=1
    )
    row_b2[0:1, :] = jnp.concatenate(
        [
            e_b[c, 1, i // 2 : i // 2 + 1, (i % 2) * R2 : (i % 2 + 1) * R2]
            for i in range(N2)
            for c in range(2)
        ],
        axis=1,
    )
    arrive_1(3)
    arrive_2(4)
    arrive_2(5)
    pass_on(9)
    arrive_1(4)
    pass_on(10)
    for k in range(4):
        sib_1[k][1].wait_recv()
    pull(0, ROWS, gb1, row_b1, 0, 8 * R)
    pass_on(11)
    arrive_2(6)
    arrive_2(7)
    arrive_1(5)
    for i in range(6):
        sib_2[i][1].wait_recv()
    pull(0, ROWS, gb2, row_b2, 0, 12 * R2)
    arrive_2(8)
    arrive_2(9)
    for k in range(4, 6):
        sib_1[k][1].wait_recv()
    pull(0, ROWS, gb1, row_b1, 8 * R, 4 * R)
    arrive_2(10)
    arrive_2(11)
    for i in range(6, 10):
        sib_2[i][1].wait_recv()
    pull(0, ROWS, gb2, row_b2, 12 * R2, 8 * R2)
    for i in range(10, 12):
        sib_2[i][1].wait_recv()
    pull(0, ROWS, gb2, row_b2, 20 * R2, 4 * R2)

    for t in range(TILES):
        partial[t].wait_recv()
        at = rows(t * T, T)
        inv = invs[at, 0:1]
        normed = emb[at, :] * inv
        unit = INV_TEMP * (acc[at, :] + part_in[at, :].astype(jnp.float32))
        radial = jnp.sum(normed * unit, axis=1, keepdims=True)
        out_ref[at, :] = inv * (unit - normed * radial)

    for copies in (own_pair, own_outer, own_behind, own_ahead, fwd, rel, rel_out, partial, e_copies):
        for copy in copies:
            copy.wait_send()
    for copies in (sib_a, sib_1, sib_2):
        for copy, _ in copies:
            copy.wait_send()
    for copy in (e_sib, e_fwd, e_rel, e_out, e_sibb, sib_own, sib_pair):
        copy.wait_send()


def solution(mesh):
    blocks = mesh.shape["blk"]
    bf16, f32 = jnp.bfloat16, jnp.float32
    dma = pltpu.SemaphoreType.DMA

    def per_device(embeddings, normalizers, partner_index):
        return pl.pallas_call(
            functools.partial(kernel, blocks),
            out_shape=jax.ShapeDtypeStruct((ROWS, D), f32),
            in_specs=[pl.BlockSpec(memory_space=pltpu.HBM)] * 3,
            out_specs=pl.BlockSpec(memory_space=pltpu.VMEM),
            scratch_shapes=[
                pltpu.VMEM((ROWS, D), f32),
                pltpu.VMEM((ROWS,), bf16),
                pltpu.VMEM((ROWS,), jnp.int32),
                pltpu.VMEM((ROWS, 128), f32),
                pltpu.VMEM((2 * ROWS, D), bf16),
                pltpu.VMEM((2, ROWS, D), bf16),
                pltpu.VMEM((6 * ROWS, D), bf16),
                pltpu.VMEM((2 * ROWS, D), bf16),
                pltpu.VMEM((2 * ROWS, D), bf16),
                pltpu.VMEM((ROWS, D), bf16),
                pltpu.VMEM((2 * ROWS, D), f32),
                pltpu.VMEM((ROWS, D), bf16),
                pltpu.VMEM((ROWS, D), bf16),
                pltpu.VMEM((8, 128), f32),
                pltpu.VMEM((8, 128), f32),
                pltpu.VMEM((2, 3, 8, 128), f32),
                pltpu.VMEM((8, 128), f32),
                pltpu.VMEM((2, 2, 8, 128), f32),
                pltpu.VMEM((2 * ROWS, 128), f32),
                pltpu.VMEM((8, 6 * ROWS), f32),
                pltpu.VMEM((8, 2 * ROWS), f32),
                pltpu.VMEM((8, 2 * ROWS), f32),
                dma((K,)), dma((2,)), dma((2,)), dma((2,)), dma((4, K)), dma((4, K)),
                dma((K,)), dma((K,)), dma((K,)), dma((K,)), dma((N2,)), dma((N2,)),
                dma((N2,)), dma((N2,)), dma((K,)), dma((K,)), dma((N2,)), dma((N2,)),
                dma((TILES,)), dma((TILES,)), dma((9,)), dma((9,)),
            ],
            compiler_params=pltpu.CompilerParams(
                collective_id=0, has_side_effects=True, vmem_limit_bytes=48 << 20
            ),
            cost_estimate=pl.CostEstimate(
                flops=10 * 10**9, bytes_accessed=4 << 20, transcendentals=3 * 10**6
            ),
        )(*[pltpu.with_memory_space_constraint(a, pltpu.HBM) for a in (embeddings, normalizers, partner_index)])

    placed = (P(("blk", "grp"), None), P(("blk", "grp")), P(("blk", "grp")))
    return jax.shard_map(
        per_device, mesh=mesh, in_specs=placed, out_specs=P(("blk", "grp"), None), check_vma=False
    )
```

```python
import functools

import jax
import jax.numpy as jnp
from jax import lax
from jax.experimental import pallas as pl
from jax.experimental.pallas import tpu as pltpu
from jax.sharding import PartitionSpec as P

MESH = pl.DeviceIdType.MESH
ROWS = 384
D = 1024
K = 6
R = ROWS // K
N2 = 12
R2 = ROWS // N2
NP = 3
T = 128
TILES = ROWS // T
INV_TEMP = 10.0
SCALE = INV_TEMP * 1.4426950408889634


def tile_of(row):
    pieces = [row[:, k * R : (k + 1) * R] for k in range(K)]
    body = jnp.concatenate(pieces + [jnp.zeros((8 - K, R), row.dtype)], axis=0)
    return jnp.concatenate([body, jnp.zeros((8, 128 - R), row.dtype)], axis=1)


def columns_of(tile):
    turned = jnp.transpose(jnp.concatenate([tile] * 16, axis=0))
    return jnp.concatenate(
        [jnp.broadcast_to(turned[0:R, k : k + 1], (R, 128)) for k in range(K)], axis=0
    )


def kernel(
    blocks, emb_hbm, norm_hbm, partner_hbm, out_ref,
    emb, norm, partner, invs, work, others, ga, gb, relay, acc, part_out, part_in,
    e_own, e_pair, e_a, e_relay, e_b, col, row_a, row_b,
    load_s, small_s, sib_s, sib_r, own_s, own_r, siba_s, siba_r, fwd_s, fwd_r, rel_s, rel_r,
    out_s, out_r, sib1_s, sib1_r, sib2_s, sib2_r, part_s, part_r, e_s, e_r,
):
    blk = lax.axis_index("blk")
    grp = lax.axis_index("grp")
    x_hi = blk % 2
    x_lo = grp // 2
    core = grp % 2
    turn = 2 * (1 - 2 * x_hi)
    pair_grp = (1 - x_lo) * 2 + core
    sib_grp = x_lo * 2 + 1 - core
    cross_grp = (1 - x_lo) * 2 + 1 - core
    sib = (blk, sib_grp)
    pair = (blk, pair_grp)
    outer = (blk + 1 - 2 * x_hi, pair_grp)
    ahead = ((blk + turn + blocks) % blocks, grp)
    behind = ((blk - turn + blocks) % blocks, grp)

    def remote(src, dst, send, recv, to):
        return pltpu.make_async_remote_copy(
            src_ref=src, dst_ref=dst, send_sem=send, recv_sem=recv, device_id=to, device_id_type=MESH
        )

    def rows(at, n):
        return pl.ds(at, n)

    def laned(at, c, n):
        return pl.ds(pl.multiple_of(at + c * n, 16), n)

    def lane_a(k, stream):
        return pl.ds(pl.multiple_of((k * 6 + stream + core * 3) * R, 16), R)

    loads = [
        pltpu.make_async_copy(emb_hbm.at[rows(k * R, R)], emb.at[rows(k * R, R)], load_s.at[k])
        for k in range(K)
    ]
    small = [
        pltpu.make_async_copy(norm_hbm, norm, small_s.at[0]),
        pltpu.make_async_copy(partner_hbm, partner, small_s.at[1]),
    ]
    small[0].start()
    for copy in loads:
        copy.start()
    small[1].start()
    barrier = pltpu.get_barrier_semaphore()
    neighbours = (sib, pair, outer, ahead, behind)
    for to in neighbours:
        pl.semaphore_signal(barrier, inc=1, device_id=to, device_id_type=MESH)

    small[0].wait()
    e_tile = tile_of(jnp.exp(-norm[...].astype(jnp.float32)).reshape(1, ROWS))
    e_own[...] = e_tile

    def normalize(k):
        loads[k].wait()
        at = rows(k * R, R)
        x = emb[at, :]
        inv = lax.rsqrt(jnp.sum(x * x, axis=1, keepdims=True) + 1e-06)
        invs[at, :] = jnp.broadcast_to(inv, (R, 128))
        work[at, :] = (x * inv).astype(jnp.bfloat16)

    e_copies = [
        remote(e_own, e_pair, e_s.at[0], e_r.at[0], pair),
        remote(e_own, e_a.at[core, 0], e_s.at[1], e_r.at[1], outer),
        remote(e_own, e_a.at[core, 1], e_s.at[2], e_r.at[2], behind),
        remote(e_own, e_a.at[core, 2], e_s.at[3], e_r.at[3], ahead),
    ]
    e_sib = remote(e_a.at[core], e_a.at[core], e_s.at[4], e_r.at[4], sib)
    e_sib_in = remote(e_a.at[1 - core], e_a.at[1 - core], e_s.at[4], e_r.at[4], sib)
    e_fwd = remote(e_a.at[core, 0], e_b.at[core, 0], e_s.at[5], e_r.at[5], ahead)
    e_rel = remote(e_pair, e_relay, e_s.at[6], e_r.at[6], behind)
    e_out = remote(e_relay, e_b.at[core, 1], e_s.at[7], e_r.at[7], outer)
    e_sibb = remote(e_b.at[core], e_b.at[core], e_s.at[8], e_r.at[8], sib)
    e_sibb_in = remote(e_b.at[1 - core], e_b.at[1 - core], e_s.at[8], e_r.at[8], sib)

    own_pair = [
        remote(work.at[rows(k * R, R)], work.at[rows(ROWS + k * R, R)], own_s.at[0, k], own_r.at[0, k], pair)
        for k in range(K)
    ]

    def own_to(stream, to):
        return [
            remote(
                work.at[rows(k * R, R)], ga.at[lane_a(k, stream)],
                own_s.at[1 + stream, k], own_r.at[1 + stream, k], to,
            )
            for k in range(K)
        ]

    own_outer, own_behind, own_ahead = own_to(0, outer), own_to(1, behind), own_to(2, ahead)

    def both_ways(ref, at, n, send, recv):
        mine = ref.at[laned(at, core, n)]
        theirs = ref.at[laned(at, 1 - core, n)]
        return remote(mine, mine, send, recv, sib), remote(theirs, theirs, send, recv, sib)

    sib_a = [both_ways(ga, k * 6 * R, 3 * R, siba_s.at[k], siba_r.at[k]) for k in range(K)]
    at_1 = [k * 2 * R + (0 if k < 4 else 8 * R) for k in range(K)]
    at_2 = [i * 2 * R2 + (8 * R if i < 8 else 12 * R) for i in range(N2)]
    sib_1 = [both_ways(gb, at_1[k], R, sib1_s.at[k], sib1_r.at[k]) for k in range(K)]
    sib_2 = [both_ways(gb, at_2[i], R2, sib2_s.at[i], sib2_r.at[i]) for i in range(N2)]
    fwd = [
        remote(
            ga.at[lane_a(k, 0)],
            gb.at[laned(at_1[k], core, R)], fwd_s.at[k], fwd_r.at[k], ahead,
        )
        for k in range(K)
    ]

    def lane_rel(i):
        return pl.ds(pl.multiple_of((i // 2 * 6 + 1 + core * 3) * R + i % 2 * R2, 16), R2)

    rel = [
        remote(
            ga.at[lane_rel(i)] if i < NP else work.at[rows(ROWS + i * R2, R2)],
            relay.at[rows(i * R2, R2)], rel_s.at[i], rel_r.at[i], pair if i < NP else behind,
        )
        for i in range(N2)
    ]
    rel_out = [
        remote(relay.at[rows(i * R2, R2)], gb.at[laned(at_2[i], core, R2)], out_s.at[i], out_r.at[i], outer)
        for i in range(N2)
    ]
    partial = [
        remote(part_out.at[rows(t * T, T)], part_in.at[rows(t * T, T)], part_s.at[t], part_r.at[t], pair)
        for t in range(TILES)
    ]
    sib_own = remote(work.at[rows(0, ROWS)], others.at[0], sib_s.at[0], sib_r.at[0], sib)
    sib_pair = remote(work.at[rows(ROWS, ROWS)], others.at[1], sib_s.at[1], sib_r.at[1], sib)

    normalize(0)
    pl.semaphore_wait(barrier, len(neighbours))
    for copy in e_copies:
        copy.start()
    for k in range(K):
        if k < 4:
            own_pair[k].start()
        own_outer[k].start()
        own_behind[k].start()
        own_ahead[k].start()
        if k + 1 < K:
            normalize(k + 1)
    sib_own.start()
    col[0:ROWS, :] = columns_of(e_tile)

    small[1].wait()
    local = partner[...].reshape(1, ROWS) - blk * (4 * ROWS)
    local = columns_of(tile_of(local.astype(jnp.float32))).astype(jnp.int32)

    def positive(held, g, first=False):
        lanes = lax.broadcasted_iota(jnp.int32, (ROWS, ROWS), 1) + g * ROWS
        spread = jnp.concatenate([local] * (ROWS // 128), axis=1)
        chosen = jnp.where(spread == lanes, -2.0, 0.0).astype(jnp.bfloat16)
        add = jnp.dot(chosen, held[...], preferred_element_type=jnp.float32)
        acc[0:ROWS, :] = add if first else acc[0:ROWS, :] + add

    positive(work.at[rows(0, ROWS)], grp, first=True)
    acc[ROWS : ROWS + T, :] = jnp.zeros((T, D), jnp.float32)

    for copy in e_copies:
        copy.wait_recv()
    e_sib.start()
    e_fwd.start()
    e_rel.start()
    col[ROWS : 2 * ROWS, :] = columns_of(e_pair[...])
    e_sib_in.wait_recv()
    row_a[0:1, :] = jnp.concatenate(
        [e_a[c, s, k : k + 1, 0:R] for k in range(K) for c in range(2) for s in range(3)], axis=1
    )

    def pull(r0, m, guests, row, g0, g, first=False):
        own, met = rows(r0, m), guests[rows(g0, g), :]
        scores = lax.dot_general(
            work[own, :], met, (((1,), (1,)), ((), ())), preferred_element_type=jnp.float32
        )
        spread = jnp.concatenate([col[own, :]] * (g // 128), axis=1) + row[0:1, g0 : g0 + g]
        weights = (jnp.exp2(scores * SCALE) * spread).astype(jnp.bfloat16)
        add = jnp.dot(weights, met, preferred_element_type=jnp.float32)
        acc[own, :] = add if first else acc[own, :] + add

    def pull_a(r0, m, k, n, first=False):
        pull(r0, m, ga, row_a, k * 6 * R, n * 6 * R, first)

    p0, p1, p2 = ROWS, ROWS + T, ROWS + 2 * T

    def arrive(k):
        own_outer[k].wait_recv()
        fwd[k].start()
        own_behind[k].wait_recv()
        for i in (2 * k, 2 * k + 1):
            if i < NP:
                rel[i].start()
        if k == 1:
            own_pair[4].start()
            own_pair[5].start()
        own_ahead[k].wait_recv()
        sib_a[k][0].start()
        if k < 4:
            arrive_pair(k)

    def arrive_pair(k):
        own_pair[k].wait_recv()
        for i in (2 * k, 2 * k + 1):
            if i >= NP:
                rel[i].start()

    def send_partial(t):
        part_out[rows(t * T, T), :] = acc[rows(ROWS + t * T, T), :].astype(jnp.bfloat16)
        partial[t].start()

    def pass_on(i):
        rel[i].wait_recv()
        rel_out[i].start()

    arrive(0)
    sib_own.wait_recv()
    positive(others.at[0], sib_grp)
    arrive(1)
    sib_a[0][1].wait_recv()
    sib_a[1][1].wait_recv()
    pull_a(0, ROWS + T, 0, 2)
    arrive(2)
    arrive(3)
    pull_a(p1, T, 0, 2, first=True)
    pass_on(0)
    sib_a[2][1].wait_recv()
    sib_a[3][1].wait_recv()
    pass_on(1)
    arrive(4)
    pull_a(0, ROWS + 2 * T, 2, 2)
    arrive(5)
    pass_on(2)
    pass_on(3)
    sib_a[4][1].wait_recv()
    pull_a(p0, 2 * T, 4, 1)
    pass_on(4)
    sib_a[5][1].wait_recv()
    pull_a(p0, 2 * T, 5, 1)
    send_partial(0)
    send_partial(1)
    pass_on(5)
    e_rel.wait_recv()
    e_out.start()
    arrive_pair(4)
    pass_on(6)
    pull_a(0, ROWS, 4, 2)
    pass_on(7)
    arrive_pair(5)
    sib_pair.start()
    pull_a(p2, T, 0, 2, first=True)
    pass_on(8)
    pull_a(p2, T, 2, 2)
    pass_on(9)
    pull_a(p2, T, 4, 2)
    send_partial(2)
    pass_on(10)
    sib_pair.wait_recv()
    positive(work.at[rows(ROWS, ROWS)], pair_grp)
    positive(others.at[1], cross_grp)
    pass_on(11)

    def arrive_1(k):
        fwd[k].wait_recv()
        sib_1[k][0].start()

    def arrive_2(i):
        rel_out[i].wait_recv()
        sib_2[i][0].start()

    e_fwd.wait_recv()
    e_out.wait_recv()
    e_sibb.start()
    for k in range(4):
        arrive_1(k)
    for i in range(8):
        arrive_2(i)
    e_sibb_in.wait_recv()
    first = [e_b[c, 0, k : k + 1, 0:R] for k in range(K) for c in range(2)]
    second = [
        e_b[c, 1, i // 2 : i // 2 + 1, (i % 2) * R2 : (i % 2 + 1) * R2] for i in range(N2) for c in range(2)
    ]
    row_b[0:1, :] = jnp.concatenate(first[:8] + second[:16] + first[8:] + second[16:], axis=1)

    for k in range(4):
        sib_1[k][1].wait_recv()
    pull(0, ROWS, gb, row_b, 0, 8 * R)
    arrive_2(8)
    arrive_2(9)
    arrive_1(4)
    for i in range(8):
        sib_2[i][1].wait_recv()
    pull(0, ROWS, gb, row_b, 8 * R, 8 * R)
    arrive_2(10)
    arrive_2(11)
    arrive_1(5)
    for k in range(4, K):
        sib_1[k][1].wait_recv()
    for i in range(8, N2):
        sib_2[i][1].wait_recv()
    pull(0, ROWS, gb, row_b, 16 * R, 8 * R)

    for t in range(TILES):
        partial[t].wait_recv()
        at = rows(t * T, T)
        inv = invs[at, 0:1]
        normed = emb[at, :] * inv
        unit = INV_TEMP * (acc[at, :] + part_in[at, :].astype(jnp.float32))
        radial = jnp.sum(normed * unit, axis=1, keepdims=True)
        out_ref[at, :] = inv * (unit - normed * radial)

    for copies in (own_pair, own_outer, own_behind, own_ahead, fwd, rel, rel_out, partial, e_copies):
        for copy in copies:
            copy.wait_send()
    for copies in (sib_a, sib_1, sib_2):
        for copy, _ in copies:
            copy.wait_send()
    for copy in (e_sib, e_fwd, e_rel, e_out, e_sibb, sib_own, sib_pair):
        copy.wait_send()


def solution(mesh):
    blocks = mesh.shape["blk"]
    bf16, f32 = jnp.bfloat16, jnp.float32
    dma = pltpu.SemaphoreType.DMA

    def per_device(embeddings, normalizers, partner_index):
        return pl.pallas_call(
            functools.partial(kernel, blocks),
            out_shape=jax.ShapeDtypeStruct((ROWS, D), f32),
            in_specs=[pl.BlockSpec(memory_space=pltpu.HBM)] * 3,
            out_specs=pl.BlockSpec(memory_space=pltpu.VMEM),
            scratch_shapes=[
                pltpu.VMEM((ROWS, D), f32),
                pltpu.VMEM((ROWS,), bf16),
                pltpu.VMEM((ROWS,), jnp.int32),
                pltpu.VMEM((ROWS, 128), f32),
                pltpu.VMEM((2 * ROWS, D), bf16),
                pltpu.VMEM((2, ROWS, D), bf16),
                pltpu.VMEM((6 * ROWS, D), bf16),
                pltpu.VMEM((4 * ROWS, D), bf16),
                pltpu.VMEM((ROWS, D), bf16),
                pltpu.VMEM((2 * ROWS, D), f32),
                pltpu.VMEM((ROWS, D), bf16),
                pltpu.VMEM((ROWS, D), bf16),
                pltpu.VMEM((8, 128), f32),
                pltpu.VMEM((8, 128), f32),
                pltpu.VMEM((2, 3, 8, 128), f32),
                pltpu.VMEM((8, 128), f32),
                pltpu.VMEM((2, 2, 8, 128), f32),
                pltpu.VMEM((2 * ROWS, 128), f32),
                pltpu.VMEM((8, 6 * ROWS), f32),
                pltpu.VMEM((8, 4 * ROWS), f32),
                dma((K,)), dma((2,)), dma((2,)), dma((2,)), dma((4, K)), dma((4, K)),
                dma((K,)), dma((K,)), dma((K,)), dma((K,)), dma((N2,)), dma((N2,)),
                dma((N2,)), dma((N2,)), dma((K,)), dma((K,)), dma((N2,)), dma((N2,)),
                dma((TILES,)), dma((TILES,)), dma((9,)), dma((9,)),
            ],
            compiler_params=pltpu.CompilerParams(
                collective_id=0, has_side_effects=True, vmem_limit_bytes=48 << 20
            ),
            cost_estimate=pl.CostEstimate(
                flops=10 * 10**9, bytes_accessed=4 << 20, transcendentals=3 * 10**6
            ),
        )(*[pltpu.with_memory_space_constraint(a, pltpu.HBM) for a in (embeddings, normalizers, partner_index)])

    placed = (P(("blk", "grp"), None), P(("blk", "grp")), P(("blk", "grp")))
    return jax.shard_map(
        per_device, mesh=mesh, in_specs=placed, out_specs=P(("blk", "grp"), None), check_vma=False
    )
```

```python
import functools

import jax
import jax.numpy as jnp
from jax import lax
from jax.experimental import pallas as pl
from jax.experimental.pallas import tpu as pltpu
from jax.sharding import PartitionSpec as P

MESH = pl.DeviceIdType.MESH
ROWS = 384
D = 1024
K = 6
R = ROWS // K
N2 = 12
R2 = ROWS // N2
NP = 3
T = 128
TILES = ((0, T), (T, T), (2 * T, T // 2), (2 * T + T // 2, T // 2))
INV_TEMP = 10.0
SCALE = INV_TEMP * 1.4426950408889634


def tile_of(row):
    pieces = [row[:, k * R : (k + 1) * R] for k in range(K)]
    body = jnp.concatenate(pieces + [jnp.zeros((8 - K, R), row.dtype)], axis=0)
    return jnp.concatenate([body, jnp.zeros((8, 128 - R), row.dtype)], axis=1)


def columns_of(tile):
    turned = jnp.transpose(jnp.concatenate([tile] * 16, axis=0))
    return jnp.concatenate(
        [jnp.broadcast_to(turned[0:R, k : k + 1], (R, 128)) for k in range(K)], axis=0
    )


def kernel(
    blocks, emb_hbm, norm_hbm, partner_hbm, out_ref,
    emb, norm, partner, invs, work, others, ga, gb, relay, acc, part_out, part_in,
    e_own, e_pair, e_a, e_relay, e_b, col, row_a, row_b,
    load_s, small_s, sib_s, sib_r, own_s, own_r, siba_s, siba_r, fwd_s, fwd_r, rel_s, rel_r,
    out_s, out_r, sib1_s, sib1_r, sib2_s, sib2_r, part_s, part_r, e_s, e_r,
):
    blk = lax.axis_index("blk")
    grp = lax.axis_index("grp")
    x_hi = blk % 2
    x_lo = grp // 2
    core = grp % 2
    turn = 2 * (1 - 2 * x_hi)
    pair_grp = (1 - x_lo) * 2 + core
    sib_grp = x_lo * 2 + 1 - core
    cross_grp = (1 - x_lo) * 2 + 1 - core
    sib = (blk, sib_grp)
    pair = (blk, pair_grp)
    outer = (blk + 1 - 2 * x_hi, pair_grp)
    ahead = ((blk + turn + blocks) % blocks, grp)
    behind = ((blk - turn + blocks) % blocks, grp)

    def remote(src, dst, send, recv, to):
        return pltpu.make_async_remote_copy(
            src_ref=src, dst_ref=dst, send_sem=send, recv_sem=recv, device_id=to, device_id_type=MESH
        )

    def rows(at, n):
        return pl.ds(at, n)

    def laned(at, c, n):
        return pl.ds(pl.multiple_of(at + c * n, 16), n)

    def lane_a(k, stream):
        return pl.ds(pl.multiple_of((k * 6 + stream + core * 3) * R, 16), R)

    loads = [
        pltpu.make_async_copy(emb_hbm.at[rows(k * R, R)], emb.at[rows(k * R, R)], load_s.at[k])
        for k in range(K)
    ]
    small = [
        pltpu.make_async_copy(norm_hbm, norm, small_s.at[0]),
        pltpu.make_async_copy(partner_hbm, partner, small_s.at[1]),
    ]
    small[0].start()
    for copy in loads:
        copy.start()
    small[1].start()
    barrier = pltpu.get_barrier_semaphore()
    neighbours = (sib, pair, outer, ahead, behind)
    for to in neighbours:
        pl.semaphore_signal(barrier, inc=1, device_id=to, device_id_type=MESH)

    small[0].wait()
    e_tile = tile_of(jnp.exp(-norm[...].astype(jnp.float32)).reshape(1, ROWS))
    e_own[...] = e_tile

    def normalize(k):
        loads[k].wait()
        at = rows(k * R, R)
        x = emb[at, :]
        inv = lax.rsqrt(jnp.sum(x * x, axis=1, keepdims=True) + 1e-06)
        invs[at, :] = jnp.broadcast_to(inv, (R, 128))
        work[at, :] = (x * inv).astype(jnp.bfloat16)

    e_copies = [
        remote(e_own, e_pair, e_s.at[0], e_r.at[0], pair),
        remote(e_own, e_a.at[core, 0], e_s.at[1], e_r.at[1], outer),
        remote(e_own, e_a.at[core, 1], e_s.at[2], e_r.at[2], behind),
        remote(e_own, e_a.at[core, 2], e_s.at[3], e_r.at[3], ahead),
    ]
    e_sib = remote(e_a.at[core], e_a.at[core], e_s.at[4], e_r.at[4], sib)
    e_sib_in = remote(e_a.at[1 - core], e_a.at[1 - core], e_s.at[4], e_r.at[4], sib)
    e_fwd = remote(e_a.at[core, 0], e_b.at[core, 0], e_s.at[5], e_r.at[5], ahead)
    e_rel = remote(e_pair, e_relay, e_s.at[6], e_r.at[6], behind)
    e_out = remote(e_relay, e_b.at[core, 1], e_s.at[7], e_r.at[7], outer)
    e_sibb = remote(e_b.at[core], e_b.at[core], e_s.at[8], e_r.at[8], sib)
    e_sibb_in = remote(e_b.at[1 - core], e_b.at[1 - core], e_s.at[8], e_r.at[8], sib)

    own_pair = [
        remote(work.at[rows(k * R, R)], work.at[rows(ROWS + k * R, R)], own_s.at[0, k], own_r.at[0, k], pair)
        for k in range(K)
    ]

    def own_to(stream, to):
        return [
            remote(
                work.at[rows(k * R, R)], ga.at[lane_a(k, stream)],
                own_s.at[1 + stream, k], own_r.at[1 + stream, k], to,
            )
            for k in range(K)
        ]

    own_outer, own_behind, own_ahead = own_to(0, outer), own_to(1, behind), own_to(2, ahead)

    def both_ways(ref, at, n, send, recv):
        mine = ref.at[laned(at, core, n)]
        theirs = ref.at[laned(at, 1 - core, n)]
        return remote(mine, mine, send, recv, sib), remote(theirs, theirs, send, recv, sib)

    sib_a = [both_ways(ga, k * 6 * R, 3 * R, siba_s.at[k], siba_r.at[k]) for k in range(K)]
    at_1 = [k * 2 * R + (0 if k < 4 else 8 * R) for k in range(K)]
    at_2 = [i * 2 * R2 + (8 * R if i < 8 else 12 * R) for i in range(N2)]
    sib_1 = [both_ways(gb, at_1[k], R, sib1_s.at[k], sib1_r.at[k]) for k in range(K)]
    sib_2 = [both_ways(gb, at_2[i], R2, sib2_s.at[i], sib2_r.at[i]) for i in range(N2)]
    fwd = [
        remote(
            ga.at[lane_a(k, 0)],
            gb.at[laned(at_1[k], core, R)], fwd_s.at[k], fwd_r.at[k], ahead,
        )
        for k in range(K)
    ]

    def lane_rel(i):
        return pl.ds(pl.multiple_of((i // 2 * 6 + 1 + core * 3) * R + i % 2 * R2, 16), R2)

    rel = [
        remote(
            ga.at[lane_rel(i)] if i < NP else work.at[rows(ROWS + i * R2, R2)],
            relay.at[rows(i * R2, R2)], rel_s.at[i], rel_r.at[i], pair if i < NP else behind,
        )
        for i in range(N2)
    ]
    rel_out = [
        remote(relay.at[rows(i * R2, R2)], gb.at[laned(at_2[i], core, R2)], out_s.at[i], out_r.at[i], outer)
        for i in range(N2)
    ]
    partial = [
        remote(part_out.at[rows(*at)], part_in.at[rows(*at)], part_s.at[t], part_r.at[t], pair)
        for t, at in enumerate(TILES)
    ]
    sib_own = remote(work.at[rows(0, ROWS)], others.at[0], sib_s.at[0], sib_r.at[0], sib)
    sib_pair = remote(work.at[rows(ROWS, ROWS)], others.at[1], sib_s.at[1], sib_r.at[1], sib)

    normalize(0)
    pl.semaphore_wait(barrier, len(neighbours))
    for copy in e_copies:
        copy.start()
    for k in range(K):
        if k < 4:
            own_pair[k].start()
        own_outer[k].start()
        own_behind[k].start()
        own_ahead[k].start()
        if k + 1 < K:
            normalize(k + 1)
    sib_own.start()
    col[0:ROWS, :] = columns_of(e_tile)

    small[1].wait()
    local = partner[...].reshape(1, ROWS) - blk * (4 * ROWS)
    local = columns_of(tile_of(local.astype(jnp.float32))).astype(jnp.int32)

    def positive(held, g, first=False):
        lanes = lax.broadcasted_iota(jnp.int32, (ROWS, ROWS), 1) + g * ROWS
        spread = jnp.concatenate([local] * (ROWS // 128), axis=1)
        chosen = jnp.where(spread == lanes, -2.0, 0.0).astype(jnp.bfloat16)
        add = jnp.dot(chosen, held[...], preferred_element_type=jnp.float32)
        acc[0:ROWS, :] = add if first else acc[0:ROWS, :] + add

    positive(work.at[rows(0, ROWS)], grp, first=True)
    acc[ROWS : ROWS + T, :] = jnp.zeros((T, D), jnp.float32)

    for copy in e_copies:
        copy.wait_recv()
    e_sib.start()
    e_fwd.start()
    e_rel.start()
    col[ROWS : 2 * ROWS, :] = columns_of(e_pair[...])
    e_sib_in.wait_recv()
    row_a[0:1, :] = jnp.concatenate(
        [e_a[c, s, k : k + 1, 0:R] for k in range(K) for c in range(2) for s in range(3)], axis=1
    )

    def pull_rows(r0, m, met, row, first=False):
        own, g = rows(r0, m), met.shape[0]
        scores = lax.dot_general(
            work[own, :], met, (((1,), (1,)), ((), ())), preferred_element_type=jnp.float32
        )
        wide = [col[own, :]] * (g // 128) + ([col[own, 0 : g % 128]] if g % 128 else [])
        spread = jnp.concatenate(wide, axis=1) + row
        weights = (jnp.exp2(scores * SCALE) * spread).astype(jnp.bfloat16)
        add = jnp.dot(weights, met, preferred_element_type=jnp.float32)
        acc[own, :] = add if first else acc[own, :] + add

    def pull(r0, m, guests, row, g0, g, first=False):
        pull_rows(r0, m, guests[rows(g0, g), :], row[0:1, g0 : g0 + g], first)

    def pull_last(r0, m, c):
        row = jnp.concatenate([e_a[c, s, K - 1 : K, 0:R] for s in range(3)], axis=1)
        pull_rows(r0, m, ga[laned((K - 1) * 6 * R, c, 3 * R), :], row)

    def pull_a(r0, m, k, n, first=False):
        pull(r0, m, ga, row_a, k * 6 * R, n * 6 * R, first)

    p0, p1, p2 = ROWS, ROWS + T, ROWS + 2 * T

    def arrive(k):
        own_outer[k].wait_recv()
        fwd[k].start()
        own_behind[k].wait_recv()
        for i in (2 * k, 2 * k + 1):
            if i < NP:
                rel[i].start()
        if k == 1:
            own_pair[4].start()
            own_pair[5].start()
        own_ahead[k].wait_recv()
        sib_a[k][0].start()
        if k < 4:
            arrive_pair(k)

    def arrive_pair(k):
        own_pair[k].wait_recv()
        for i in (2 * k, 2 * k + 1):
            if i >= NP:
                rel[i].start()

    def send_partial(t):
        at, n = TILES[t]
        part_out[rows(at, n), :] = acc[rows(ROWS + at, n), :].astype(jnp.bfloat16)
        partial[t].start()

    def pass_on(i):
        rel[i].wait_recv()
        rel_out[i].start()

    arrive(0)
    sib_own.wait_recv()
    positive(others.at[0], sib_grp)
    arrive(1)
    sib_a[0][1].wait_recv()
    sib_a[1][1].wait_recv()
    pull_a(0, ROWS + T, 0, 2)
    arrive(2)
    arrive(3)
    pull_a(p1, T, 0, 2, first=True)
    pass_on(0)
    sib_a[2][1].wait_recv()
    sib_a[3][1].wait_recv()
    pass_on(1)
    arrive(4)
    pull_a(p0, 2 * T, 2, 2)
    pass_on(2)
    pull_a(0, ROWS, 2, 1)
    arrive(5)
    pass_on(3)
    sib_a[4][1].wait_recv()
    pull_a(p0, 2 * T, 4, 1)
    pull_last(p0, 2 * T, core)
    pass_on(4)
    sib_a[5][1].wait_recv()
    pull_last(p0, 2 * T, 1 - core)
    send_partial(0)
    send_partial(1)
    pass_on(5)
    e_rel.wait_recv()
    e_out.start()
    arrive_pair(4)
    pass_on(6)
    pull_a(0, ROWS, 3, 3)
    pass_on(7)
    arrive_pair(5)
    sib_pair.start()
    pull_a(p2, T, 0, 2, first=True)
    pass_on(8)
    pull_a(p2, T, 2, 2)
    pass_on(9)
    pull_a(p2, T, 4, 2)
    send_partial(2)
    send_partial(3)
    pass_on(10)
    sib_pair.wait_recv()
    positive(work.at[rows(ROWS, ROWS)], pair_grp)
    positive(others.at[1], cross_grp)
    pass_on(11)

    def arrive_1(k):
        fwd[k].wait_recv()
        sib_1[k][0].start()

    def arrive_2(i):
        rel_out[i].wait_recv()
        sib_2[i][0].start()

    e_fwd.wait_recv()
    e_out.wait_recv()
    e_sibb.start()
    for k in range(4):
        arrive_1(k)
    for i in range(8):
        arrive_2(i)
    e_sibb_in.wait_recv()
    first = [e_b[c, 0, k : k + 1, 0:R] for k in range(K) for c in range(2)]
    second = [
        e_b[c, 1, i // 2 : i // 2 + 1, (i % 2) * R2 : (i % 2 + 1) * R2] for i in range(N2) for c in range(2)
    ]
    row_b[0:1, :] = jnp.concatenate(first[:8] + second[:16] + first[8:] + second[16:], axis=1)

    for k in range(4):
        sib_1[k][1].wait_recv()
    pull(0, ROWS, gb, row_b, 0, 8 * R)
    arrive_2(8)
    arrive_2(9)
    arrive_1(4)
    for i in range(8):
        sib_2[i][1].wait_recv()
    pull(0, ROWS, gb, row_b, 8 * R, 8 * R)
    arrive_2(10)
    arrive_2(11)
    arrive_1(5)
    for k in range(4, K):
        sib_1[k][1].wait_recv()
    for i in range(8, N2):
        sib_2[i][1].wait_recv()
    pull(0, ROWS, gb, row_b, 16 * R, 8 * R)

    def finish(t):
        partial[t].wait_recv()
        at = rows(*TILES[t])
        inv = invs[at, 0:1]
        normed = emb[at, :] * inv
        unit = INV_TEMP * (acc[at, :] + part_in[at, :].astype(jnp.float32))
        radial = jnp.sum(normed * unit, axis=1, keepdims=True)
        out_ref[at, :] = inv * (unit - normed * radial)

    finish(0)
    finish(1)
    for copies in (own_pair, own_outer, own_behind, own_ahead, fwd, rel, rel_out, partial[:2], e_copies):
        for copy in copies:
            copy.wait_send()
    for copies in (sib_a, sib_1, sib_2):
        for copy, _ in copies:
            copy.wait_send()
    for copy in (e_sib, e_fwd, e_rel, e_out, e_sibb, sib_own, sib_pair):
        copy.wait_send()
    finish(2)
    finish(3)
    for copy in partial[2:]:
        copy.wait_send()


def solution(mesh):
    blocks = mesh.shape["blk"]
    bf16, f32 = jnp.bfloat16, jnp.float32
    dma = pltpu.SemaphoreType.DMA

    def per_device(embeddings, normalizers, partner_index):
        return pl.pallas_call(
            functools.partial(kernel, blocks),
            out_shape=jax.ShapeDtypeStruct((ROWS, D), f32),
            in_specs=[pl.BlockSpec(memory_space=pltpu.HBM)] * 3,
            out_specs=pl.BlockSpec(memory_space=pltpu.VMEM),
            scratch_shapes=[
                pltpu.VMEM((ROWS, D), f32),
                pltpu.VMEM((ROWS,), bf16),
                pltpu.VMEM((ROWS,), jnp.int32),
                pltpu.VMEM((ROWS, 128), f32),
                pltpu.VMEM((2 * ROWS, D), bf16),
                pltpu.VMEM((2, ROWS, D), bf16),
                pltpu.VMEM((6 * ROWS, D), bf16),
                pltpu.VMEM((4 * ROWS, D), bf16),
                pltpu.VMEM((ROWS, D), bf16),
                pltpu.VMEM((2 * ROWS, D), f32),
                pltpu.VMEM((ROWS, D), bf16),
                pltpu.VMEM((ROWS, D), bf16),
                pltpu.VMEM((8, 128), f32),
                pltpu.VMEM((8, 128), f32),
                pltpu.VMEM((2, 3, 8, 128), f32),
                pltpu.VMEM((8, 128), f32),
                pltpu.VMEM((2, 2, 8, 128), f32),
                pltpu.VMEM((2 * ROWS, 128), f32),
                pltpu.VMEM((8, 6 * ROWS), f32),
                pltpu.VMEM((8, 4 * ROWS), f32),
                dma((K,)), dma((2,)), dma((2,)), dma((2,)), dma((4, K)), dma((4, K)),
                dma((K,)), dma((K,)), dma((K,)), dma((K,)), dma((N2,)), dma((N2,)),
                dma((N2,)), dma((N2,)), dma((K,)), dma((K,)), dma((N2,)), dma((N2,)),
                dma((len(TILES),)), dma((len(TILES),)), dma((9,)), dma((9,)),
            ],
            compiler_params=pltpu.CompilerParams(
                collective_id=0, has_side_effects=True, vmem_limit_bytes=48 << 20
            ),
            cost_estimate=pl.CostEstimate(
                flops=10 * 10**9, bytes_accessed=4 << 20, transcendentals=3 * 10**6
            ),
        )(*[pltpu.with_memory_space_constraint(a, pltpu.HBM) for a in (embeddings, normalizers, partner_index)])

    placed = (P(("blk", "grp"), None), P(("blk", "grp")), P(("blk", "grp")))
    return jax.shard_map(
        per_device, mesh=mesh, in_specs=placed, out_specs=P(("blk", "grp"), None), check_vma=False
    )
```

```python
import functools

import jax
import jax.numpy as jnp
from jax import lax
from jax.experimental import pallas as pl
from jax.experimental.pallas import tpu as pltpu
from jax.sharding import PartitionSpec as P

MESH = pl.DeviceIdType.MESH
ROWS = 384
D = 1024
K = 6
R = ROWS // K
N2 = 12
R2 = ROWS // N2
NP = 3
T = 128
TILES = ((0, T), (T, T), (2 * T, T // 2), (2 * T + T // 2, T // 2))
INV_TEMP = 10.0
SCALE = INV_TEMP * 1.4426950408889634


def tile_of(row):
    pieces = [row[:, k * R : (k + 1) * R] for k in range(K)]
    body = jnp.concatenate(pieces + [jnp.zeros((8 - K, R), row.dtype)], axis=0)
    return jnp.concatenate([body, jnp.zeros((8, 128 - R), row.dtype)], axis=1)


def columns_of(tile):
    turned = jnp.transpose(jnp.concatenate([tile] * 16, axis=0))
    return jnp.concatenate(
        [jnp.broadcast_to(turned[0:R, k : k + 1], (R, 128)) for k in range(K)], axis=0
    )


def kernel(
    blocks, emb_hbm, norm_hbm, partner_hbm, out_ref,
    emb, norm, partner, invs, work, others, ga, gb, relay, acc, part_out, part_in,
    e_own, e_pair, e_a, e_relay, e_b, col, row_a, row_b,
    load_s, small_s, sib_s, sib_r, own_s, own_r, siba_s, siba_r, fwd_s, fwd_r, rel_s, rel_r,
    out_s, out_r, sib1_s, sib1_r, sib2_s, sib2_r, part_s, part_r, e_s, e_r,
):
    blk = lax.axis_index("blk")
    grp = lax.axis_index("grp")
    x_hi = blk % 2
    x_lo = grp // 2
    core = grp % 2
    turn = 2 * (1 - 2 * x_hi)
    pair_grp = (1 - x_lo) * 2 + core
    sib_grp = x_lo * 2 + 1 - core
    cross_grp = (1 - x_lo) * 2 + 1 - core
    sib = (blk, sib_grp)
    pair = (blk, pair_grp)
    outer = (blk + 1 - 2 * x_hi, pair_grp)
    ahead = ((blk + turn + blocks) % blocks, grp)
    behind = ((blk - turn + blocks) % blocks, grp)

    def remote(src, dst, send, recv, to):
        return pltpu.make_async_remote_copy(
            src_ref=src, dst_ref=dst, send_sem=send, recv_sem=recv, device_id=to, device_id_type=MESH
        )

    def rows(at, n):
        return pl.ds(at, n)

    def laned(at, c, n):
        return pl.ds(pl.multiple_of(at + c * n, 16), n)

    def lane_a(k, stream):
        return pl.ds(pl.multiple_of((k * 6 + stream + core * 3) * R, 16), R)

    loads = [
        pltpu.make_async_copy(emb_hbm.at[rows(k * R, R)], emb.at[rows(k * R, R)], load_s.at[k])
        for k in range(K)
    ]
    small = [
        pltpu.make_async_copy(norm_hbm, norm, small_s.at[0]),
        pltpu.make_async_copy(partner_hbm, partner, small_s.at[1]),
    ]
    small[0].start()
    for copy in loads:
        copy.start()
    small[1].start()
    barrier = pltpu.get_barrier_semaphore()
    neighbours = (sib, pair, outer, ahead, behind)
    for to in neighbours:
        pl.semaphore_signal(barrier, inc=1, device_id=to, device_id_type=MESH)

    small[0].wait()
    e_tile = tile_of(jnp.exp(-norm[...].astype(jnp.float32)).reshape(1, ROWS))
    e_own[...] = e_tile

    def normalize(k):
        loads[k].wait()
        at = rows(k * R, R)
        x = emb[at, :]
        inv = lax.rsqrt(jnp.sum(x * x, axis=1, keepdims=True) + 1e-06)
        invs[at, :] = jnp.broadcast_to(inv, (R, 128))
        work[at, :] = (x * inv).astype(jnp.bfloat16)

    e_copies = [
        remote(e_own, e_pair, e_s.at[0], e_r.at[0], pair),
        remote(e_own, e_a.at[core, 0], e_s.at[1], e_r.at[1], outer),
        remote(e_own, e_a.at[core, 1], e_s.at[2], e_r.at[2], behind),
        remote(e_own, e_a.at[core, 2], e_s.at[3], e_r.at[3], ahead),
    ]
    e_sib = remote(e_a.at[core], e_a.at[core], e_s.at[4], e_r.at[4], sib)
    e_sib_in = remote(e_a.at[1 - core], e_a.at[1 - core], e_s.at[4], e_r.at[4], sib)
    e_fwd = remote(e_a.at[core, 0], e_b.at[core, 0], e_s.at[5], e_r.at[5], ahead)
    e_rel = remote(e_pair, e_relay, e_s.at[6], e_r.at[6], behind)
    e_out = remote(e_relay, e_b.at[core, 1], e_s.at[7], e_r.at[7], outer)
    e_sibb = remote(e_b.at[core], e_b.at[core], e_s.at[8], e_r.at[8], sib)
    e_sibb_in = remote(e_b.at[1 - core], e_b.at[1 - core], e_s.at[8], e_r.at[8], sib)

    own_pair = [
        remote(work.at[rows(k * R, R)], work.at[rows(ROWS + k * R, R)], own_s.at[0, k], own_r.at[0, k], pair)
        for k in range(K)
    ]

    def own_to(stream, to):
        return [
            remote(
                work.at[rows(k * R, R)], ga.at[lane_a(k, stream)],
                own_s.at[1 + stream, k], own_r.at[1 + stream, k], to,
            )
            for k in range(K)
        ]

    own_outer, own_behind, own_ahead = own_to(0, outer), own_to(1, behind), own_to(2, ahead)

    def both_ways(ref, at, n, send, recv):
        mine = ref.at[laned(at, core, n)]
        theirs = ref.at[laned(at, 1 - core, n)]
        return remote(mine, mine, send, recv, sib), remote(theirs, theirs, send, recv, sib)

    sib_a = [both_ways(ga, k * 6 * R, 3 * R, siba_s.at[k], siba_r.at[k]) for k in range(K - 1)]

    def last_ways(stream):
        mine, theirs = (
            ga.at[pl.ds(pl.multiple_of(((K - 1) * 6 + stream + c * 3) * R, 16), R)] for c in (core, 1 - core)
        )
        send, recv = siba_s.at[K - 1 + stream], siba_r.at[K - 1 + stream]
        return remote(mine, mine, send, recv, sib), remote(theirs, theirs, send, recv, sib)

    sib_last = [last_ways(stream) for stream in range(3)]
    at_1 = [k * 2 * R + (0 if k < 4 else 8 * R) for k in range(K)]
    at_2 = [i * 2 * R2 + (8 * R if i < 8 else 12 * R) for i in range(N2)]
    sib_1 = [both_ways(gb, at_1[k], R, sib1_s.at[k], sib1_r.at[k]) for k in range(K)]
    sib_2 = [both_ways(gb, at_2[i], R2, sib2_s.at[i], sib2_r.at[i]) for i in range(N2)]
    fwd = [
        remote(
            ga.at[lane_a(k, 0)],
            gb.at[laned(at_1[k], core, R)], fwd_s.at[k], fwd_r.at[k], ahead,
        )
        for k in range(K)
    ]

    def lane_rel(i):
        return pl.ds(pl.multiple_of((i // 2 * 6 + 1 + core * 3) * R + i % 2 * R2, 16), R2)

    rel = [
        remote(
            ga.at[lane_rel(i)] if i < NP else work.at[rows(ROWS + i * R2, R2)],
            relay.at[rows(i * R2, R2)], rel_s.at[i], rel_r.at[i], pair if i < NP else behind,
        )
        for i in range(N2)
    ]
    rel_out = [
        remote(relay.at[rows(i * R2, R2)], gb.at[laned(at_2[i], core, R2)], out_s.at[i], out_r.at[i], outer)
        for i in range(N2)
    ]
    partial = [
        remote(part_out.at[rows(*at)], part_in.at[rows(*at)], part_s.at[t], part_r.at[t], pair)
        for t, at in enumerate(TILES)
    ]
    sib_own = remote(work.at[rows(0, ROWS)], others.at[0], sib_s.at[0], sib_r.at[0], sib)
    sib_pair = remote(work.at[rows(ROWS, ROWS)], others.at[1], sib_s.at[1], sib_r.at[1], sib)

    normalize(0)
    pl.semaphore_wait(barrier, len(neighbours))
    for copy in e_copies:
        copy.start()
    for k in range(K):
        if k < 4:
            own_pair[k].start()
        own_outer[k].start()
        own_behind[k].start()
        own_ahead[k].start()
        if k + 1 < K:
            normalize(k + 1)
    sib_own.start()
    col[0:ROWS, :] = columns_of(e_tile)

    small[1].wait()
    local = partner[...].reshape(1, ROWS) - blk * (4 * ROWS)
    local = columns_of(tile_of(local.astype(jnp.float32))).astype(jnp.int32)

    def positive(held, g, first=False):
        lanes = lax.broadcasted_iota(jnp.int32, (ROWS, ROWS), 1) + g * ROWS
        spread = jnp.concatenate([local] * (ROWS // 128), axis=1)
        chosen = jnp.where(spread == lanes, -2.0, 0.0).astype(jnp.bfloat16)
        add = jnp.dot(chosen, held[...], preferred_element_type=jnp.float32)
        acc[0:ROWS, :] = add if first else acc[0:ROWS, :] + add

    positive(work.at[rows(0, ROWS)], grp, first=True)
    acc[ROWS : ROWS + T, :] = jnp.zeros((T, D), jnp.float32)

    for copy in e_copies:
        copy.wait_recv()
    e_sib.start()
    e_fwd.start()
    e_rel.start()
    col[ROWS : 2 * ROWS, :] = columns_of(e_pair[...])
    e_sib_in.wait_recv()
    row_a[0:1, :] = jnp.concatenate(
        [e_a[c, s, k : k + 1, 0:R] for k in range(K) for c in range(2) for s in range(3)], axis=1
    )

    def pull_rows(r0, m, met, row, first=False):
        own, g = rows(r0, m), met.shape[0]
        scores = lax.dot_general(
            work[own, :], met, (((1,), (1,)), ((), ())), preferred_element_type=jnp.float32
        )
        wide = [col[own, :]] * (g // 128) + ([col[own, 0 : g % 128]] if g % 128 else [])
        spread = jnp.concatenate(wide, axis=1) + row
        weights = (jnp.exp2(scores * SCALE) * spread).astype(jnp.bfloat16)
        add = jnp.dot(weights, met, preferred_element_type=jnp.float32)
        acc[own, :] = add if first else acc[own, :] + add

    def pull(r0, m, guests, row, g0, g, first=False):
        pull_rows(r0, m, guests[rows(g0, g), :], row[0:1, g0 : g0 + g], first)

    def pull_last(r0, m, c):
        row = jnp.concatenate([e_a[c, s, K - 1 : K, 0:R] for s in range(3)], axis=1)
        pull_rows(r0, m, ga[laned((K - 1) * 6 * R, c, 3 * R), :], row)

    def pull_a(r0, m, k, n, first=False):
        pull(r0, m, ga, row_a, k * 6 * R, n * 6 * R, first)

    p0, p1, p2 = ROWS, ROWS + T, ROWS + 2 * T

    def arrive(k):
        last = k == K - 1
        own_outer[k].wait_recv()
        if last:
            sib_last[0][0].start()
        fwd[k].start()
        own_behind[k].wait_recv()
        if last:
            sib_last[1][0].start()
        for i in (2 * k, 2 * k + 1):
            if i < NP:
                rel[i].start()
        if k == 1:
            own_pair[4].start()
            own_pair[5].start()
        own_ahead[k].wait_recv()
        if last:
            sib_last[2][0].start()
        else:
            sib_a[k][0].start()
        if k < 4:
            arrive_pair(k)

    def arrive_pair(k):
        own_pair[k].wait_recv()
        for i in (2 * k, 2 * k + 1):
            if i >= NP:
                rel[i].start()

    def send_partial(t):
        at, n = TILES[t]
        part_out[rows(at, n), :] = acc[rows(ROWS + at, n), :].astype(jnp.bfloat16)
        partial[t].start()

    def pass_on(i):
        rel[i].wait_recv()
        rel_out[i].start()

    arrive(0)
    sib_own.wait_recv()
    positive(others.at[0], sib_grp)
    arrive(1)
    sib_a[0][1].wait_recv()
    sib_a[1][1].wait_recv()
    pull_a(0, ROWS + T, 0, 2)
    arrive(2)
    arrive(3)
    pull_a(p1, T, 0, 2, first=True)
    pass_on(0)
    sib_a[2][1].wait_recv()
    sib_a[3][1].wait_recv()
    pass_on(1)
    arrive(4)
    pull_a(p0, 2 * T, 2, 2)
    pass_on(2)
    pull_a(0, ROWS, 2, 1)
    arrive(5)
    pass_on(3)
    sib_a[4][1].wait_recv()
    pull_a(p0, 2 * T, 4, 1)
    pull_last(p0, 2 * T, core)
    pass_on(4)
    for _, copy in sib_last:
        copy.wait_recv()
    pull_last(p0, 2 * T, 1 - core)
    send_partial(0)
    send_partial(1)
    pass_on(5)
    e_rel.wait_recv()
    e_out.start()
    arrive_pair(4)
    pass_on(6)
    pull_a(0, ROWS, 3, 3)
    pass_on(7)
    arrive_pair(5)
    sib_pair.start()
    pull_a(p2, T, 0, 2, first=True)
    pass_on(8)
    pull_a(p2, T, 2, 2)
    pass_on(9)
    pull_a(p2, T, 4, 2)
    send_partial(2)
    send_partial(3)
    pass_on(10)
    sib_pair.wait_recv()
    positive(work.at[rows(ROWS, ROWS)], pair_grp)
    positive(others.at[1], cross_grp)
    pass_on(11)

    def arrive_1(k):
        fwd[k].wait_recv()
        sib_1[k][0].start()

    def arrive_2(i):
        rel_out[i].wait_recv()
        sib_2[i][0].start()

    e_fwd.wait_recv()
    e_out.wait_recv()
    e_sibb.start()
    for k in range(4):
        arrive_1(k)
    for i in range(8):
        arrive_2(i)
    e_sibb_in.wait_recv()
    first = [e_b[c, 0, k : k + 1, 0:R] for k in range(K) for c in range(2)]
    second = [
        e_b[c, 1, i // 2 : i // 2 + 1, (i % 2) * R2 : (i % 2 + 1) * R2] for i in range(N2) for c in range(2)
    ]
    row_b[0:1, :] = jnp.concatenate(first[:8] + second[:16] + first[8:] + second[16:], axis=1)

    for k in range(4):
        sib_1[k][1].wait_recv()
    pull(0, ROWS, gb, row_b, 0, 8 * R)
    arrive_2(8)
    arrive_2(9)
    arrive_1(4)
    for i in range(8):
        sib_2[i][1].wait_recv()
    pull(0, ROWS, gb, row_b, 8 * R, 8 * R)
    arrive_2(10)
    arrive_2(11)
    arrive_1(5)
    for k in range(4, K):
        sib_1[k][1].wait_recv()
    for i in range(8, N2):
        sib_2[i][1].wait_recv()
    pull(0, ROWS, gb, row_b, 16 * R, 8 * R)

    def finish(t):
        partial[t].wait_recv()
        at = rows(*TILES[t])
        inv = invs[at, 0:1]
        normed = emb[at, :] * inv
        unit = INV_TEMP * (acc[at, :] + part_in[at, :].astype(jnp.float32))
        radial = jnp.sum(normed * unit, axis=1, keepdims=True)
        out_ref[at, :] = inv * (unit - normed * radial)

    finish(0)
    finish(1)
    for copies in (own_pair, own_outer, own_behind, own_ahead, fwd, rel, rel_out, partial[:2], e_copies):
        for copy in copies:
            copy.wait_send()
    for copies in (sib_a, sib_last, sib_1, sib_2):
        for copy, _ in copies:
            copy.wait_send()
    for copy in (e_sib, e_fwd, e_rel, e_out, e_sibb, sib_own, sib_pair):
        copy.wait_send()
    finish(2)
    finish(3)
    for copy in partial[2:]:
        copy.wait_send()


def solution(mesh):
    blocks = mesh.shape["blk"]
    bf16, f32 = jnp.bfloat16, jnp.float32
    dma = pltpu.SemaphoreType.DMA

    def per_device(embeddings, normalizers, partner_index):
        return pl.pallas_call(
            functools.partial(kernel, blocks),
            out_shape=jax.ShapeDtypeStruct((ROWS, D), f32),
            in_specs=[pl.BlockSpec(memory_space=pltpu.HBM)] * 3,
            out_specs=pl.BlockSpec(memory_space=pltpu.VMEM),
            scratch_shapes=[
                pltpu.VMEM((ROWS, D), f32),
                pltpu.VMEM((ROWS,), bf16),
                pltpu.VMEM((ROWS,), jnp.int32),
                pltpu.VMEM((ROWS, 128), f32),
                pltpu.VMEM((2 * ROWS, D), bf16),
                pltpu.VMEM((2, ROWS, D), bf16),
                pltpu.VMEM((6 * ROWS, D), bf16),
                pltpu.VMEM((4 * ROWS, D), bf16),
                pltpu.VMEM((ROWS, D), bf16),
                pltpu.VMEM((2 * ROWS, D), f32),
                pltpu.VMEM((ROWS, D), bf16),
                pltpu.VMEM((ROWS, D), bf16),
                pltpu.VMEM((8, 128), f32),
                pltpu.VMEM((8, 128), f32),
                pltpu.VMEM((2, 3, 8, 128), f32),
                pltpu.VMEM((8, 128), f32),
                pltpu.VMEM((2, 2, 8, 128), f32),
                pltpu.VMEM((2 * ROWS, 128), f32),
                pltpu.VMEM((8, 6 * ROWS), f32),
                pltpu.VMEM((8, 4 * ROWS), f32),
                dma((K,)), dma((2,)), dma((2,)), dma((2,)), dma((4, K)), dma((4, K)),
                dma((K + 2,)), dma((K + 2,)), dma((K,)), dma((K,)), dma((N2,)), dma((N2,)),
                dma((N2,)), dma((N2,)), dma((K,)), dma((K,)), dma((N2,)), dma((N2,)),
                dma((len(TILES),)), dma((len(TILES),)), dma((9,)), dma((9,)),
            ],
            compiler_params=pltpu.CompilerParams(
                collective_id=0, has_side_effects=True, vmem_limit_bytes=48 << 20
            ),
            cost_estimate=pl.CostEstimate(
                flops=10 * 10**9, bytes_accessed=4 << 20, transcendentals=3 * 10**6
            ),
        )(*[pltpu.with_memory_space_constraint(a, pltpu.HBM) for a in (embeddings, normalizers, partner_index)])

    placed = (P(("blk", "grp"), None), P(("blk", "grp")), P(("blk", "grp")))
    return jax.shard_map(
        per_device, mesh=mesh, in_specs=placed, out_specs=P(("blk", "grp"), None), check_vma=False
    )
```
